512 devices in a mesh: group: 16 (over y, core), member: 32 (over z, x).
Axes of the slice: x: 4, y: 8, z: 8, core: 2. Of those that a mesh axis runs over, the one named last changes fastest.
Arguments:
- cache: bfloat16 [2048, 512, 576], P(('group', 'member')), may hold values from -8 to 8
- cache_len: int32 [2048], P(('group', 'member')), may hold values from 1 to 512, as said below
- query: bfloat16 [2048, 2, 128, 576], P(('group', 'member')), may hold values from -32 to 32
- fresh: bfloat16 [65536, 576], P(('group', 'member')), may hold values from -4 to 4
- fresh_dest: int32 [65536, 1], P(('group', 'member')), may hold values from 0 to 15; in each aligned block of 128 rows (0 to 127, 128 to 255, ...) at most 16 rows name the same one
- fresh_slot: int32 [65536], P(('group', 'member')), may hold values from 0 to 3
- token_group: int32 [4096, 1], P('group'), may hold values from 0 to 15; in each aligned block of 256 rows (0 to 255, 256 to 511, ...) at most 32 rows name the same one
- w_uv: bfloat16 [128, 512, 128], P('member'), may hold values from -0.25 to 0.25
Outputs:
- dispatched: bfloat16 [8192, 16384], P('group', 'member')
The draws below stay inside these ranges and needn't reach their ends.
Inputs may be any that keep to these rules, and one draw needn't show every extreme that they name: `cache_len`: every request has at least one valid resident row, and some request has 512 in every draw. `fresh_dest`: of the 128 rows of one device, at most 16 name the same group; some group is named by exactly 16 rows. `token_group`: of the 256 tokens of one group, at most 32 name the same expert group; some expert group is named by exactly 32.
All inputs are finite; a program needn't handle non-finite values.
Results may differ from the reference program's by a relative error of at most 0.0057.
Values may be sent and summed in bfloat16 or wider, within the bound.
A program may use at most 64 MiB of HBM per device.

```python
import math
import jax
import jax.numpy as jnp
import numpy as np
from jax import lax

H = 128
KVL = 512
ROPE = 64
NOPE = 128
VH = 128
B = 4
QTOK = 2
LMAX = 512
FRESH = 128
REQUESTS = 2048
FRESH_TOTAL = 65536
TOK_GROUP = 256
TOKENS = 4096
CAP = 16
CAPE = 32
N_GROUP = 16
N_MEMBER = 32


def shared_rows(key):
    return jax.random.truncated_normal(key, -4.0, 4.0, (REQUESTS, LMAX, KVL + ROPE), jnp.float32)


def draw_cache(key, part):
    base = shared_rows(key)
    return base.astype(jnp.bfloat16)


def draw_query(key, part):
    key = jax.random.fold_in(key, 12)
    first = jax.random.fold_in(key, 0)
    values = jax.random.truncated_normal(first, -4.0, 4.0, (REQUESTS, QTOK, H, KVL + ROPE), jnp.float32)
    return values.astype(jnp.bfloat16)


def draw_cache_len(key, part):
    key = jax.random.fold_in(key, 13)
    first, second = jax.random.split(key)
    lengths = jax.random.randint(first, (REQUESTS,), 1, LMAX + 1)
    chosen = jax.random.randint(second, (), 0, REQUESTS)
    return lengths.at[chosen].set(LMAX).astype(jnp.int32)


def place_ends(array, stream_key, smallest, largest):
    shape = array.shape
    place = [jax.random.randint(jax.random.fold_in(stream_key, axis), (), 0, shape[axis]) for axis in range(len(shape))]
    array = array.at[tuple(place)].set(smallest)
    longest = shape.index(max(shape))
    place[longest] = (place[longest] + 1) % shape[longest]
    return array.at[tuple(place)].set(largest)


def block_levels(rng, shape, cuts, smallest, top_value):
    factor_of = 1.0
    for position, shards_of in cuts:
        steps = jax.random.uniform(jax.random.fold_in(jax.random.fold_in(rng, 6), position), (shards_of,), jnp.float32, smallest / len(cuts), top_value / len(cuts))
        factor_of = factor_of * jnp.repeat(jnp.exp(steps), shape[position] // shards_of).reshape((-1,) + (1,) * (len(shape) - 1 - position))
    return factor_of


def shared_out(key, own, number, rows, number_of, top, limit, lean):
    sequence = jax.random.permutation(key, number_of)
    crowded, common = load_shares(number_of, rows * top, limit, lean, True), load_shares(number_of, rows * top, limit, lean, False)
    places = jnp.arange(number_of)

    def named(sizes, offset_by):
        used = int((sizes > 0).sum())
        fixed = max(1, used // 4)
        shifted = fixed + (places - fixed + offset_by * (used - fixed)) % max(1, number_of - fixed)
        return jnp.zeros((number_of,), jnp.int32).at[sequence[jnp.where(places < fixed, places, shifted)]].set(jnp.asarray(sizes, jnp.int32))

    sizes = jnp.where(number % 4 == 0, named(crowded, number // 4), named(common, number - number // 4 - 1))
    mixed = jax.random.permutation(jax.random.fold_in(own, 3), number_of)
    giver, sink = mixed[0:number_of // 2 * 2:2], mixed[1:number_of // 2 * 2:2]
    margin = jnp.minimum(sizes[giver] - 1, limit - sizes[sink]) // 2
    margin = jnp.where((giver == sequence[0]) | (sink == sequence[0]) | (sizes[sink] == 0), 0, jnp.maximum(margin, 0))
    shifted = jax.random.randint(jax.random.fold_in(own, 4), (number_of // 2,), 0, 1 << 20) % (margin + 1)
    sizes = sizes.at[giver].add(-shifted).at[sink].add(shifted)
    items = jnp.searchsorted(jnp.cumsum(sizes), jnp.arange(rows * top), side="right").astype(jnp.int32)
    table = items.reshape(top, rows).T
    table = table[jax.random.permutation(jax.random.fold_in(own, 1), rows)]
    offset_by = jax.random.randint(jax.random.fold_in(own, 2), (rows, 1), 0, top)
    return jnp.take_along_axis(table, (jnp.arange(top)[None, :] + offset_by) % top, axis=1)


def load_shares(number_of, total, reach, lean, full):
    weights = [(1 << 20) // math.isqrt(rank ** lean) + 1 for rank in range(1, number_of + 1)]
    largest = reach if full else min(reach, max(-(-total // number_of), total * weights[0] // sum(weights)))
    least = 1 if total - largest >= number_of - 1 else 0
    given, spare = [largest] + [least] * (number_of - 1), total - largest - least * (number_of - 1)
    while spare > 0:
        free = [i for i in range(1, number_of) if given[i] < largest] or [i for i in range(1, number_of) if given[i] < reach]
        whole, remaining = sum([weights[i] for i in free]), spare
        for i in free:
            extra = min(reach - given[i], max(1, remaining * weights[i] // whole), spare)
            given[i] = given[i] + extra
            spare = spare - extra
    return np.array(given)


def centred(key, shape, deviation, reach, pieces=(), kind=jnp.bfloat16):
    array = deviation * jax.random.normal(key, shape, jnp.float32)
    if pieces:
        array = array * block_levels(key, shape, pieces, -0.22, 0.18)
    return jnp.clip(array, -reach, reach).astype(kind)


def setup_inputs(seed: int = 0) -> dict:
    keys = jax.random.split(jax.random.key(seed), 9)
    cache = draw_cache(jax.random.fold_in(keys[8], 71), 0)
    cache_len = draw_cache_len(jax.random.fold_in(keys[8], 71), 0)
    query = draw_query(jax.random.fold_in(keys[8], 71), 0)
    fresh = centred(keys[3], (FRESH_TOTAL, KVL + ROPE), 1.0, 4.0, ((0, 512),))
    fresh_dest_keys = jax.random.split(jax.random.fold_in(keys[4], 1), FRESH_TOTAL // FRESH)
    fresh_dest_turns = jax.random.permutation(jax.random.fold_in(keys[4], 3), FRESH_TOTAL // FRESH)
    fresh_dest = jax.vmap(lambda own, number: shared_out(jax.random.fold_in(keys[4], 2), own, number, FRESH, N_GROUP, 1, CAP, 2))(fresh_dest_keys, fresh_dest_turns).reshape((FRESH_TOTAL, 1))
    fresh_slot = place_ends(jax.random.randint(keys[5], (FRESH_TOTAL,), 0, B), jax.random.fold_in(keys[5], 1), 0, B - 1).astype(jnp.int32)
    token_group_keys = jax.random.split(jax.random.fold_in(keys[6], 1), TOKENS // TOK_GROUP)
    token_group_turns = jax.random.permutation(jax.random.fold_in(keys[6], 3), TOKENS // TOK_GROUP)
    token_group = jax.vmap(lambda own, number: shared_out(jax.random.fold_in(keys[6], 2), own, number, TOK_GROUP, N_GROUP, 1, CAPE, 2))(token_group_keys, token_group_turns).reshape((TOKENS, 1))
    w_uv = centred(keys[7], (H, KVL, VH), KVL ** -0.5, 0.25, ((0, 32),))
    return {"cache": cache, "cache_len": cache_len, "query": query, "fresh": fresh, "fresh_dest": fresh_dest, "fresh_slot": fresh_slot, "token_group": token_group, "w_uv": w_uv}


def place_rows(targets, peers, cap):
    onehot = (targets[:, None] == jnp.arange(peers, dtype=jnp.int32)[None, :]).astype(jnp.int32)
    before = jnp.sum(jnp.cumsum(onehot, 0) * onehot, 1) - 1
    return (targets * cap + before).astype(jnp.int32)


def attend(query, cache, lengths, arrived, labels):
    count = cache.shape[0]
    scale = (NOPE + ROPE) ** -0.5
    query_f = query.astype(jnp.float32)
    cache_f = cache.astype(jnp.float32)
    arrived_f = arrived.astype(jnp.float32)
    near = jnp.einsum("bqhw,blw->bqhl", query_f, cache_f) * scale
    far = jnp.einsum("bqhw,aw->bqha", query_f, arrived_f) * scale
    near_mask = (jnp.arange(cache.shape[1], dtype=jnp.int32)[None, :] < lengths[:, None])[:, None, None, :]
    far_mask = (labels[None, :] == jnp.arange(count, dtype=jnp.int32)[:, None])[:, None, None, :]
    near = jnp.where(near_mask, near, -jnp.inf)
    far = jnp.where(far_mask, far, -jnp.inf)
    top = jnp.maximum(jnp.max(near, -1, keepdims=True), jnp.max(far, -1, keepdims=True))
    near_p = jnp.exp(near - top)
    far_p = jnp.exp(far - top)
    total = jnp.sum(near_p, -1, keepdims=True) + jnp.sum(far_p, -1, keepdims=True)
    near_w = (near_p / total).astype(jnp.bfloat16).astype(jnp.float32)
    far_w = (far_p / total).astype(jnp.bfloat16).astype(jnp.float32)
    latent = jnp.einsum("bqhl,blc->bqhc", near_w, cache_f[..., :KVL])
    latent = latent + jnp.einsum("bqha,ac->bqhc", far_w, arrived_f[:, :KVL])
    return latent.astype(jnp.bfloat16)


def reference(cache, cache_len, query, fresh, fresh_dest, fresh_slot, token_group, w_uv):
    groups = N_GROUP
    members = N_MEMBER
    devices = groups * members
    width = KVL + ROPE
    dest = fresh_dest[:, 0].reshape(devices, FRESH)
    slots = fresh_slot.reshape(devices, FRESH)
    rows = fresh.reshape(devices, FRESH, width)

    def section(rows_d, dest_d, slots_d):
        where_to = place_rows(dest_d, groups, CAP)
        sectioned = jnp.zeros((groups * CAP, width), jnp.bfloat16).at[where_to].set(rows_d)
        labels = jnp.full((groups * CAP,), -1, jnp.int32).at[where_to].set(slots_d)
        return sectioned, labels

    sectioned, labels = jax.vmap(section)(rows, dest, slots)
    sectioned = sectioned.reshape(groups, members, groups, CAP, width).transpose(2, 1, 0, 3, 4)
    sectioned = sectioned.reshape(devices, groups * CAP, width)
    labels = labels.reshape(groups, members, groups, CAP).transpose(2, 1, 0, 3).reshape(devices, groups * CAP)

    w_uv_f = w_uv.astype(jnp.float32)

    def per_device(items):
        cache_d, len_d, query_d, arrived_d, labels_d = items
        latent = attend(query_d, cache_d, len_d, arrived_d, labels_d)
        lifted = jnp.einsum("bqhc,hcv->bqhv", latent.astype(jnp.float32), w_uv_f)
        return lifted.astype(jnp.bfloat16)

    lifted = lax.map(per_device, (cache.reshape(devices, B, LMAX, width), cache_len.reshape(devices, B),
                                  query.reshape(devices, B, QTOK, H, width), sectioned, labels))
    values = lifted.reshape(groups, TOK_GROUP, H * VH)
    targets = token_group[:, 0].reshape(groups, TOK_GROUP)

    def pack(values_s, targets_s):
        where_to = place_rows(targets_s, groups, CAPE)
        return jnp.zeros((groups * CAPE, H * VH), jnp.bfloat16).at[where_to].set(values_s)

    packed = jax.vmap(pack)(values, targets).reshape(groups, groups, CAPE, H * VH)
    return packed.transpose(1, 0, 2, 3).reshape(groups * groups * CAPE, H * VH)
```

```python
import jax
import jax.numpy as jnp
from jax import lax
from jax.sharding import PartitionSpec as P

KVL = 512
ROPE = 64
NOPE = 128


def place_rows(targets, peers, cap):
    onehot = (targets[:, None] == jnp.arange(peers, dtype=jnp.int32)[None, :]).astype(jnp.int32)
    before = jnp.sum(jnp.cumsum(onehot, 0) * onehot, 1) - 1
    return targets * cap + before


def attend(query, cache, lengths, arrived, labels):
    count = cache.shape[0]
    scale = (NOPE + ROPE) ** (-0.5)
    near = jnp.einsum("bqhw,blw->bqhl", query, cache, preferred_element_type=jnp.float32) * scale
    far = jnp.einsum("bqhw,aw->bqha", query, arrived, preferred_element_type=jnp.float32) * scale
    near_mask = (jnp.arange(cache.shape[1], dtype=jnp.int32)[None, :] < lengths[:, None])[
        :, None, None, :
    ]
    far_mask = (labels[None, :] == jnp.arange(count, dtype=jnp.int32)[:, None])[:, None, None, :]
    near = jnp.where(near_mask, near, -jnp.inf)
    far = jnp.where(far_mask, far, -jnp.inf)
    top = jnp.maximum(jnp.max(near, -1, keepdims=True), jnp.max(far, -1, keepdims=True))
    near_p = jnp.exp(near - top)
    far_p = jnp.exp(far - top)
    total = jnp.sum(near_p, -1, keepdims=True) + jnp.sum(far_p, -1, keepdims=True)
    near_w = (near_p / total).astype(jnp.bfloat16)
    far_w = (far_p / total).astype(jnp.bfloat16)
    latent = jnp.einsum(
        "bqhl,blc->bqhc", near_w, cache[..., :KVL], preferred_element_type=jnp.float32
    )
    latent = latent + jnp.einsum(
        "bqha,ac->bqhc", far_w, arrived[:, :KVL], preferred_element_type=jnp.float32
    )
    return latent.astype(jnp.bfloat16)


def local(cache, cache_len, query, fresh, fresh_dest, fresh_slot, token_group, w_uv):
    groups = lax.axis_size("group")
    count = cache.shape[0]
    dest = fresh_dest[:, 0]
    cap = 2 * fresh.shape[0] // groups
    where_to = place_rows(dest, groups, cap)
    marks = (fresh_slot[:, None] == jnp.arange(count, dtype=jnp.int32)[None, :]).astype(fresh.dtype)
    rows = jnp.concatenate([fresh, marks, jnp.zeros((fresh.shape[0], ROPE - count), fresh.dtype)], 1)
    picks = (where_to[None, :] == jnp.arange(groups * cap, dtype=jnp.int32)[:, None]).astype(fresh.dtype)
    packed_rows = jnp.dot(picks, rows, preferred_element_type=jnp.float32).astype(fresh.dtype)
    landed = lax.all_to_all(
        packed_rows.reshape(groups, cap, rows.shape[1]), "group", split_axis=0, concat_axis=0, tiled=True
    ).reshape(groups * cap, rows.shape[1])
    arrived = landed[:, : fresh.shape[1]]
    owned = landed[:, fresh.shape[1] : fresh.shape[1] + count]
    labels = jnp.sum(owned * jnp.arange(1, count + 1, dtype=owned.dtype)[None, :], 1).astype(jnp.int32) - 1
    latent = attend(query, cache, cache_len, arrived, labels)
    lifted = jnp.einsum(
        "bqhc,hcv->bqhv",
        lax.all_to_all(latent, "member", split_axis=2, concat_axis=0, tiled=True),
        w_uv,
        preferred_element_type=jnp.float32,
    ).astype(jnp.bfloat16)
    tok_rows = lifted.shape[0] * lifted.shape[1]
    values = lifted.reshape(tok_rows, lifted.shape[2] * lifted.shape[3])
    cape = 2 * tok_rows // groups
    where_tok = place_rows(token_group[:, 0], groups, cape)
    packed = jnp.zeros((groups * cape, values.shape[1]), jnp.bfloat16).at[where_tok].set(values)
    received = lax.all_to_all(
        packed.reshape(groups, cape, values.shape[1]),
        "group",
        split_axis=0,
        concat_axis=0,
        tiled=True,
    )
    return received.reshape(groups * cape, values.shape[1])


def solution(mesh):
    placed = (
        P(("group", "member"), None, None),
        P(("group", "member")),
        P(("group", "member"), None, None, None),
        P(("group", "member"), None),
        P(("group", "member"), None),
        P(("group", "member")),
        P("group", None),
        P("member", None, None),
    )
    return jax.shard_map(
        local, mesh=mesh, in_specs=placed, out_specs=P("group", "member"), check_vma=False
    )
```

```python
import functools

import jax
import jax.numpy as jnp
from jax import lax
from jax.experimental import pallas as pl
from jax.experimental.pallas import tpu as pltpu
from jax.sharding import PartitionSpec as P

KVL = 512
ROPE = 64
NOPE = 128
VH = 128
WIDTH = KVL + ROPE
WIDE = 640
SCALE = (NOPE + ROPE) ** (-0.5)
MESH = pl.DeviceIdType.MESH
F32 = jnp.float32
BF16 = jnp.bfloat16


def iota(shape, axis):
    return lax.broadcasted_iota(jnp.int32, shape, axis)


def swing(j, n):
    half = (j + 1) // 2
    return lax.rem(jnp.where(lax.rem(j, 2) == 1, half, n - half), n)


def group_peer(k, g, groups):
    rows = groups // 2
    y = lax.rem(g // 2 + swing(k // 2, rows), rows)
    return y * 2 + lax.rem(lax.rem(g, 2) + lax.rem(k, 2), 2)


def member_peer(k, m, members):
    rows = members // 4
    z = lax.rem(m // 4 + swing(k // 4, rows), rows)
    return z * 4 + lax.rem(lax.rem(m, 4) + lax.rem(k, 4), 4)


def one_hot_places(targets, peers, cap):
    n = targets.shape[1]
    named = iota((peers, n), 0) == targets
    earlier = (iota((n, n), 0) < iota((n, n), 1)).astype(BF16)
    counts = jnp.dot(named.astype(BF16), earlier, preferred_element_type=F32)
    slot = jnp.sum(jnp.where(named, counts, 0.0), 0, keepdims=True)
    where_to = targets * cap + slot.astype(jnp.int32)
    return (iota((peers * cap, n), 0) == where_to).astype(BF16)


def kernel(
    groups, members, lens_ref, dest_ref, slot_ref, tok_ref, fresh_ref, cache_hbm, query_hbm, w_hbm,
    out_ref,
    cache, query, weights, fresh_out, arrived, queries, top, total, near, bias, picks,
    lat_out, lat_in, disp,
    in_sem, fresh_ssem, fresh_rsem, lat_ssem, lat_rsem, disp_ssem, disp_rsem, own_sem,
):
    g, m = lax.axis_index("group"), lax.axis_index("member")
    count, keys = cache_hbm.shape[0], cache_hbm.shape[1]
    rows = query_hbm.shape[1]
    heads = w_hbm.shape[0]
    part = rows // heads
    qtok = part // members
    mine = count * qtok
    cap = fresh_out.shape[1]
    cape = disp.shape[1] // groups

    barrier = pltpu.get_barrier_semaphore()

    @pl.loop(1, groups)
    def _(k):
        pl.semaphore_signal(barrier, inc=1, device_id=(group_peer(k, g, groups), m), device_id_type=MESH)

    @pl.loop(1, members)
    def _(k):
        pl.semaphore_signal(barrier, inc=1, device_id=(g, member_peer(k, m, members)), device_id_type=MESH)

    def load_query(b):
        return pltpu.make_async_copy(query_hbm.at[b], query.at[b], in_sem.at[b])

    def load_cache(b):
        return pltpu.make_async_copy(cache_hbm.at[b], cache.at[b], in_sem.at[count + b])

    load_w = pltpu.make_async_copy(w_hbm, weights, in_sem.at[2 * count])
    for b in range(count):
        load_query(b).start()
        load_cache(b).start()
    load_w.start()

    places = one_hot_places(dest_ref[...], groups, cap)
    fresh_out[:, :, :WIDTH] = (
        jnp.dot(places, fresh_ref[...], preferred_element_type=F32)
        .astype(BF16)
        .reshape(groups, cap, WIDTH)
    )
    n = fresh_ref.shape[0]
    marks = (iota((128, n), 0) - 64 == slot_ref[...]).astype(BF16)
    marked = lax.dot_general(places, marks, (((1,), (1,)), ((), ())), preferred_element_type=F32)
    fresh_out[:, :, WIDTH:] = marked[:, 64:].astype(BF16).reshape(groups, cap, WIDE - WIDTH)

    pl.semaphore_wait(barrier, groups - 1 + members - 1)

    @pl.loop(1, groups)
    def _(k):
        e = group_peer(k, g, groups)
        pltpu.make_async_remote_copy(
            src_ref=fresh_out.at[e], dst_ref=arrived.at[g],
            send_sem=fresh_ssem.at[0], recv_sem=fresh_rsem.at[0],
            device_id=(e, m), device_id_type=MESH,
        ).start()

    arrived[g] = fresh_out[g]

    r, c = iota((rows, rows), 0), iota((rows, rows), 1)
    order = (lax.rem(r, qtok) * (rows // qtok) + lax.rem(r, part) // qtok * heads + r // part == c).astype(BF16)

    @pl.loop(0, count)
    def _(b):
        load_query(b).wait()
        load_cache(b).wait()
        q = jnp.dot(order, query[b], preferred_element_type=F32).astype(BF16)
        span = pl.ds(pl.multiple_of(b * part, part), part)
        queries[:, span, :] = q.reshape(heads, part, WIDTH)
        score = lax.dot_general(q, cache[b], (((1,), (1,)), ((), ())), preferred_element_type=F32) * SCALE
        score = jnp.where(iota((rows, keys), 1) < lens_ref[b], score, -jnp.inf)
        high = jnp.max(score, -1, keepdims=True)
        p = jnp.exp(score - high)
        top[:, span, :] = high.reshape(heads, part, 1)
        total[:, span, :] = jnp.sum(p, -1, keepdims=True).reshape(heads, part, 1)
        near[:, span, :] = jnp.dot(
            p.astype(BF16), cache[b, :, :KVL], preferred_element_type=F32
        ).reshape(heads, part, KVL)

    picks[...] = one_hot_places(tok_ref[...], groups, cape)
    load_w.wait()
    half = KVL // 2

    pltpu.make_async_copy(
        arrived.at[pl.ds(0, groups - 1)], arrived.at[pl.ds(0, groups - 1)], fresh_rsem.at[0]
    ).wait()
    pool = groups * cap
    chosen = (iota((8, 128), 1) - 64 == iota((8, 128), 0)).astype(BF16)
    labelled = lax.dot_general(
        chosen, arrived[:, :, KVL:].reshape(pool, WIDE - KVL), (((1,), (1,)), ((), ())),
        preferred_element_type=F32,
    )
    for b in range(count):
        bias[b * part : (b + 1) * part, :] = jnp.broadcast_to(
            jnp.where(labelled[b : b + 1, :] > 0.5, 0.0, -jnp.inf), (part, pool)
        )

    r, c = iota((rows, rows), 0), iota((rows, rows), 1)
    back = (lax.rem(r, mine) // qtok * part + r // mine * qtok + lax.rem(r, qtok) == c).astype(BF16)

    @pl.loop(0, heads)
    def _(h):
        keys_in = arrived[...].reshape(pool, WIDE)
        score = lax.dot_general(
            queries[h], keys_in[:, :WIDTH], (((1,), (1,)), ((), ())), preferred_element_type=F32
        )
        score = score * SCALE + bias[...]
        high = jnp.maximum(top[h], jnp.max(score, -1, keepdims=True))
        p = jnp.exp(score - high)
        shrink = jnp.exp(top[h] - high)
        norm = 1.0 / (total[h] * shrink + jnp.sum(p, -1, keepdims=True))
        far = jnp.dot(p.astype(BF16), keys_in[:, :KVL], preferred_element_type=F32)
        latent = ((near[h] * shrink + far) * norm).astype(BF16)
        moved = jnp.dot(back, latent, preferred_element_type=F32).reshape(members, mine, KVL)
        lat_out[h] = jnp.concatenate([moved[:, :, :half], moved[:, :, half:]], 1).astype(BF16)

        @pl.loop(1, members)
        def _(k):
            d = member_peer(k, m, members)
            pltpu.make_async_remote_copy(
                src_ref=lat_out.at[h, d], dst_ref=lat_in.at[h, m],
                send_sem=lat_ssem.at[h], recv_sem=lat_rsem.at[h],
                device_id=(g, d), device_id_type=MESH,
            ).start()

        lat_in[h, m] = lat_out[h, m]

    @pl.loop(0, heads)
    def _(h):
        pltpu.make_async_copy(
            lat_in.at[h, pl.ds(0, members - 1)], lat_in.at[h, pl.ds(0, members - 1)], lat_rsem.at[h]
        ).wait()
        w = jnp.concatenate([weights[h, :half, :], weights[h, half:, :]], 1)
        both = jnp.dot(
            lat_in[h].reshape(members * 2 * mine, half), w, preferred_element_type=F32
        ).reshape(members, 2 * mine, 2 * VH)
        value = (both[:, :mine, :VH] + both[:, mine:, VH:]).reshape(members * mine, VH).astype(BF16)
        disp[h] = jnp.dot(picks[...], value, preferred_element_type=F32).astype(BF16)
        columns = pl.ds(pl.multiple_of(h * VH, VH), VH)
        spot = out_ref.at[pl.ds(pl.multiple_of(g * cape, cape), cape), columns]

        @pl.loop(1, groups)
        def _(k):
            e = group_peer(k, g, groups)
            pltpu.make_async_remote_copy(
                src_ref=disp.at[h, pl.ds(pl.multiple_of(e * cape, cape), cape)], dst_ref=spot,
                send_sem=disp_ssem.at[h], recv_sem=disp_rsem.at[h],
                device_id=(e, m), device_id_type=MESH,
            ).start()

        pltpu.make_async_copy(
            disp.at[h, pl.ds(pl.multiple_of(g * cape, cape), cape)], spot, own_sem.at[h]
        ).start()

    def wait_for(ref, sem):
        pltpu.make_async_copy(ref, ref, sem).wait()

    wait_for(fresh_out.at[pl.ds(0, groups - 1)], fresh_ssem.at[0])

    @pl.loop(0, heads)
    def _(h):
        wait_for(lat_out.at[h, pl.ds(0, members - 1)], lat_ssem.at[h])
        wait_for(disp.at[h, pl.ds(0, (groups - 1) * cape)], disp_ssem.at[h])
        wait_for(disp.at[h, pl.ds(0, (groups - 1) * cape)], disp_rsem.at[h])
        wait_for(disp.at[h, pl.ds(0, cape)], own_sem.at[h])


def local(cache, cache_len, query, fresh, fresh_dest, fresh_slot, token_group, w_uv):
    groups, members = lax.axis_size("group"), lax.axis_size("member")
    count, qtok, all_heads = query.shape[:3]
    rows = qtok * all_heads
    heads = w_uv.shape[0]
    n = fresh.shape[0]
    cap = 2 * n // groups
    tokens = token_group.shape[0]
    cape = 2 * tokens // groups
    mine = count * qtok
    vmem = pl.BlockSpec(memory_space=pltpu.VMEM)
    anywhere = pl.BlockSpec(memory_space=pl.ANY)
    dma = pltpu.SemaphoreType.DMA
    return pl.pallas_call(
        functools.partial(kernel, groups, members),
        out_shape=jax.ShapeDtypeStruct((groups * cape, heads * VH), BF16),
        in_specs=[pl.BlockSpec(memory_space=pltpu.SMEM), vmem, vmem, vmem, vmem, anywhere, anywhere, anywhere],
        out_specs=anywhere,
        scratch_shapes=[
            pltpu.VMEM(cache.shape, BF16),
            pltpu.VMEM((count, rows, WIDTH), BF16),
            pltpu.VMEM(w_uv.shape, BF16),
            pltpu.VMEM((groups, cap, WIDE), BF16),
            pltpu.VMEM((groups, cap, WIDE), BF16),
            pltpu.VMEM((heads, rows * count // heads, WIDTH), BF16),
            pltpu.VMEM((heads, rows * count // heads, 1), F32),
            pltpu.VMEM((heads, rows * count // heads, 1), F32),
            pltpu.VMEM((heads, rows * count // heads, KVL), F32),
            pltpu.VMEM((rows * count // heads, groups * cap), F32),
            pltpu.VMEM((groups * cape, tokens), BF16),
            pltpu.VMEM((heads, members, 2 * mine, KVL // 2), BF16),
            pltpu.VMEM((heads, members, 2 * mine, KVL // 2), BF16),
            pltpu.VMEM((heads, groups * cape, VH), BF16),
            dma((2 * count + 1,)),
            dma((1,)),
            dma((1,)),
            dma((heads,)),
            dma((heads,)),
            dma((heads,)),
            dma((heads,)),
            dma((heads,)),
        ],
        compiler_params=pltpu.CompilerParams(
            collective_id=0, has_side_effects=True, vmem_limit_bytes=48 * 1024 * 1024
        ),
        cost_estimate=pl.CostEstimate(flops=2_500_000_000, bytes_accessed=6_000_000, transcendentals=800_000),
    )(
        cache_len,
        fresh_dest.reshape(1, n),
        fresh_slot.reshape(1, n),
        token_group.reshape(1, tokens),
        fresh,
        cache,
        query.reshape(count, rows, WIDTH),
        w_uv,
    )


def solution(mesh):
    placed = (
        P(("group", "member"), None, None),
        P(("group", "member")),
        P(("group", "member"), None, None, None),
        P(("group", "member"), None),
        P(("group", "member"), None),
        P(("group", "member")),
        P("group", None),
        P("member", None, None),
    )
    return jax.shard_map(
        local, mesh=mesh, in_specs=placed, out_specs=P("group", "member"), check_vma=False
    )
```

```python
import functools

import jax
import jax.numpy as jnp
from jax import lax
from jax.experimental import pallas as pl
from jax.experimental.pallas import tpu as pltpu
from jax.sharding import PartitionSpec as P

KVL = 512
ROPE = 64
NOPE = 128
VH = 128
WIDTH = KVL + ROPE
WIDE = 640
SCALE = (NOPE + ROPE) ** (-0.5)
MESH = pl.DeviceIdType.MESH
F32 = jnp.float32
BF16 = jnp.bfloat16
REACH = 2
NT = (((1,), (1,)), ((), ()))


def iota(shape, axis):
    return lax.broadcasted_iota(jnp.int32, shape, axis)


def swing(j):
    return ((j + 1) >> 1) * (2 * (j & 1) - 1)


def group_peer(k, g, groups):
    return ((((g >> 1) + swing(k >> 1)) & (groups // 2 - 1)) << 1) | ((g ^ k) & 1)


def one_hot_places(targets, peers, cap):
    n = targets.shape[1]
    named = iota((peers, n), 0) == targets
    earlier = (iota((n, n), 0) < iota((n, n), 1)).astype(BF16)
    counts = jnp.dot(named.astype(BF16), earlier, preferred_element_type=F32)
    slot = jnp.sum(jnp.where(named, counts, 0.0), 0, keepdims=True)
    where_to = targets * cap + slot.astype(jnp.int32)
    return (iota((peers * cap, n), 0) == where_to).astype(BF16)


def kernel(
    groups, members, lens_hbm, dest_hbm, slot_hbm, tok_hbm, fresh_hbm, cache_hbm, query_hbm, w_hbm,
    out_ref,
    lens, dest, slot, tok, fresh, cache, query, weights, fresh_out, arrived, queries, top, total, near,
    bias, picks, back, lat_out, lat_in, val_out, val_in, disp,
    in_sem, fresh_ssem, fresh_rsem, ring_ssem, ring_rsem, twin_ssem, twin_rsem,
    lat_ssem, lat_rsem, side_ssem, side_rsem, val_ssem, val_rsem, disp_ssem, disp_rsem, own_sem,
):
    g, m = lax.axis_index("group"), lax.axis_index("member")
    count, keys = cache_hbm.shape[0], cache_hbm.shape[2]
    qtok = query_hbm.shape[1]
    rows = qtok * query_hbm.shape[3]
    heads = w_hbm.shape[0]
    part = rows // heads
    mine = count * qtok
    cap = fresh_out.shape[1]
    cape = disp.shape[1] // groups
    nx = 4
    nz = members // nx
    z, x, core = m >> 2, m & 3, g & 1
    half = KVL // 2
    pair = heads // 2

    def at_z(k):
        return (((z + k) & (nz - 1)) << 2) | x

    def at_x(k):
        return (z << 2) | ((x + k) & 3)

    def load(src, dst, i):
        return pltpu.make_async_copy(src, dst, in_sem.at[i])

    small = [
        load(fresh_hbm, fresh, 0), load(dest_hbm, dest, 1), load(slot_hbm, slot, 2),
        load(tok_hbm, tok, 3), load(lens_hbm, lens, 4),
    ]
    load_w = load(w_hbm, weights.at[REACH], 5)
    queries_in = [load(query_hbm.at[b], query.at[b], 6 + b) for b in range(count)]
    cache_in = [load(cache_hbm.at[b], cache.at[b], 6 + count + b) for b in range(count)]
    for copy in small:
        copy.start()

    barrier = pltpu.get_barrier_semaphore()

    @pl.loop(1, groups)
    def _(k):
        pl.semaphore_signal(barrier, inc=1, device_id=(group_peer(k, g, groups), m), device_id_type=MESH)

    @pl.loop(1, nz)
    def _(k):
        pl.semaphore_signal(barrier, inc=1, device_id=(g, at_z(k)), device_id_type=MESH)

    @pl.loop(1, nx)
    def _(k):
        pl.semaphore_signal(barrier, inc=1, device_id=(g, at_x(k)), device_id_type=MESH)
        for step in (-2, -1, 1, 2):
            aside = (at_z(step) & ~3) | ((x + k) & 3)
            pl.semaphore_signal(barrier, inc=1, device_id=(g, aside), device_id_type=MESH)

    load_w.start()
    for b in range(count):
        queries_in[b].start()
        cache_in[b].start()
    for copy in small:
        copy.wait()

    places = one_hot_places(dest[...], groups, cap)
    fresh_out[:, :, :WIDTH] = (
        lax.dot_general(places, fresh[...], NT, preferred_element_type=F32)
        .astype(BF16)
        .reshape(groups, cap, WIDTH)
    )
    n = fresh.shape[1]
    marks = (iota((128, n), 0) - 64 == slot[...]).astype(BF16)
    marked = lax.dot_general(places, marks, NT, preferred_element_type=F32)
    fresh_out[:, :, WIDTH:] = marked[:, 64:].astype(BF16).reshape(groups, cap, WIDE - WIDTH)

    pl.semaphore_wait(barrier, groups - 1 + nz - 1 + 5 * (nx - 1))

    @pl.loop(1, groups)
    def _(k):
        e = group_peer(groups - k, g, groups)
        pltpu.make_async_remote_copy(
            src_ref=fresh_out.at[e], dst_ref=arrived.at[g],
            send_sem=fresh_ssem.at[0], recv_sem=fresh_rsem.at[0],
            device_id=(e, m), device_id_type=MESH,
        ).start()

    arrived[g] = fresh_out[g]

    def piece(k, ab, side):
        return weights.at[
            REACH + k, pl.ds(ab * pair, pair), pl.ds(pl.multiple_of(side * half, half), half)
        ]

    def ring_copy(step, way, ab):
        sign = 1 - 2 * way
        return pltpu.make_async_remote_copy(
            src_ref=piece(-sign * (step - 1), ab, core), dst_ref=piece(-sign * step, ab, core),
            send_sem=ring_ssem.at[step - 1, way, ab], recv_sem=ring_rsem.at[step - 1, way, ab],
            device_id=(g, at_z(sign)), device_id_type=MESH,
        )

    def twin_copy(step, way, ab):
        sign = 1 - 2 * way
        return pltpu.make_async_remote_copy(
            src_ref=piece(-sign * step, ab, core), dst_ref=piece(-sign * step, ab, core),
            send_sem=twin_ssem.at[step - 1, way, ab], recv_sem=twin_rsem.at[step - 1, way, ab],
            device_id=(g ^ 1, m), device_id_type=MESH,
        )

    def wait_for(ref, sem):
        pltpu.make_async_copy(ref, ref, sem).wait()

    def ring_pass(step, ab):
        for way in range(2):
            here = piece(-(1 - 2 * way) * step, ab, core)
            wait_for(here, ring_rsem.at[step - 1, way, ab])
            if step < REACH:
                ring_copy(step + 1, way, ab).start()
            twin_copy(step, way, ab).start()

    def twin_wait(ab):
        for step in range(1, REACH + 1):
            for way in range(2):
                there = piece(-(1 - 2 * way) * step, ab, 1 - core)
                wait_for(there, twin_rsem.at[step - 1, way, ab])

    load_w.wait()
    for ab in range(2):
        for way in range(2):
            ring_copy(1, way, ab).start()

    r, c = iota((rows, rows), 0), iota((rows, rows), 1)
    order = (lax.rem(r, qtok) * (rows // qtok) + lax.rem(r, part) // qtok * heads + r // part == c).astype(BF16)
    for b in range(count):
        queries_in[b].wait()
        cache_in[b].wait()
        columns = jnp.concatenate([query[b, i] for i in range(qtok)], 1)
        q = lax.dot_general(order, columns, NT, preferred_element_type=F32).astype(BF16)
        span = pl.ds(b * part, part)
        queries[:, span, :] = q.reshape(heads, part, WIDTH)
        score = jnp.dot(q, cache[b], preferred_element_type=F32) * SCALE
        score = jnp.where(iota((rows, keys), 1) < lens[b], score, -jnp.inf)
        high = jnp.max(score, -1, keepdims=True)
        p = jnp.exp(score - high)
        top[:, span, :] = high.reshape(heads, part, 1)
        total[:, span, :] = jnp.sum(p, -1, keepdims=True).reshape(heads, part, 1)
        near[:, span, :] = lax.dot_general(
            p.astype(BF16), cache[b, :KVL, :], NT, preferred_element_type=F32
        ).reshape(heads, part, KVL)

    picks[...] = one_hot_places(tok[...], groups, cape)
    r, c = iota((rows, rows), 0), iota((rows, rows), 1)
    whose = ((r // mine + z + nz // 2) & (nz - 1)) * nx + r // (mine * nz)
    back[...] = (lax.rem(r, mine) // qtok * part + whose * qtok + lax.rem(r, qtok) == c).astype(BF16)

    for ab in range(2):
        ring_pass(1, ab)

    wait_for(arrived.at[pl.ds(0, groups - 1)], fresh_rsem.at[0])
    pool = groups * cap
    chosen = (iota((8, 128), 1) - 64 == iota((8, 128), 0)).astype(BF16)
    labelled = lax.dot_general(
        chosen, arrived[:, :, KVL:].reshape(pool, WIDE - KVL), NT,
        preferred_element_type=F32,
    )
    for b in range(count):
        bias[b * part : (b + 1) * part, :] = jnp.broadcast_to(
            jnp.where(labelled[b : b + 1, :] > 0.5, 0.0, -jnp.inf), (part, pool)
        )

    def attend(h):
        keys_in = arrived[...].reshape(pool, WIDE)
        score = lax.dot_general(queries[h], keys_in[:, :WIDTH], NT, preferred_element_type=F32)
        score = score * SCALE + bias[...]
        high = jnp.maximum(top[h], jnp.max(score, -1, keepdims=True))
        p = jnp.exp(score - high)
        shrink = jnp.exp(top[h] - high)
        norm = 1.0 / (total[h] * shrink + jnp.sum(p, -1, keepdims=True))
        far = jnp.dot(p.astype(BF16), keys_in[:, :KVL], preferred_element_type=F32)
        latent = ((near[h] * shrink + far) * norm).astype(BF16)
        moved = jnp.dot(back[...], latent, preferred_element_type=F32).reshape(nx, nz, mine, KVL)
        lat_out[h] = jnp.concatenate([moved[..., :half], moved[..., half:]], 2).astype(BF16)

    near_slots = 2 * REACH + 1

    def far_way(h):
        return 1 - 2 * (h & 1)

    def send_latents(h):
        @pl.loop(0, nx)
        def _(k):
            to = (x + k) & 3
            for source, slot, step in ((0, 7, 2 * far_way(h)), (7, 5, 1), (1, 6, -1)):
                pltpu.make_async_remote_copy(
                    src_ref=lat_out.at[h, to, source], dst_ref=lat_in.at[h, x, slot],
                    send_sem=side_ssem.at[h], recv_sem=side_rsem.at[h],
                    device_id=(g, (((z + step) & (nz - 1)) << 2) | to), device_id_type=MESH,
                ).start()

        for k in (2, 1, 3):
            pltpu.make_async_remote_copy(
                src_ref=lat_out.at[h, (x + k) & 3, pl.ds(2, near_slots)],
                dst_ref=lat_in.at[h, x, pl.ds(0, near_slots)],
                send_sem=lat_ssem.at[h], recv_sem=lat_rsem.at[h],
                device_id=(g, at_x(k)), device_id_type=MESH,
            ).start()

        lat_in[h, x, :near_slots] = lat_out[h, x, 2 : 2 + near_slots]

    def project(h):
        wait_for(lat_in.at[h, pl.ds(0, nx - 1), pl.ds(0, near_slots)], lat_rsem.at[h])
        wait_for(lat_in.at[h, pl.ds(0, nx), pl.ds(0, 3)], side_rsem.at[h])
        way = far_way(h)
        plan = [(k, 0) for k in range(-REACH, REACH + 1)] + [(2, -1), (-2, 1), (2 * way, -2 * way)]
        for k in (REACH, -REACH, 1, -1, 0):
            slots = [i for i, (owner, _) in enumerate(plan) if owner == k]
            w = jnp.concatenate([weights[REACH + k, h, :half, :], weights[REACH + k, h, half:, :]], 1)
            taken = [lat_in[h, :, i].reshape(nx * 2 * mine, half) for i in slots]
            both = jnp.dot(
                jnp.concatenate(taken, 0), w, preferred_element_type=F32
            ).reshape(len(slots), nx, 2 * mine, 2 * VH)
            value = both[:, :, :mine, :VH] + both[:, :, mine:, VH:]
            for j, i in enumerate(slots):
                block = value[j].reshape(nx * mine, VH).astype(BF16)
                if k == 0:
                    val_in[h, z] = block
                    continue
                val_out[h, i] = block
                pltpu.make_async_remote_copy(
                    src_ref=val_out.at[h, i], dst_ref=val_in.at[h, (z + plan[i][1]) & (nz - 1)],
                    send_sem=val_ssem.at[h], recv_sem=val_rsem.at[h],
                    device_id=(g, at_z(k)), device_id_type=MESH,
                ).start()

    def dispatch(h):
        wait_for(val_in.at[h, pl.ds(0, nz - 1)], val_rsem.at[h])
        value = val_in[h].reshape(members * mine, VH)
        disp[h] = jnp.dot(picks[...], value, preferred_element_type=F32).astype(BF16)
        spot = out_ref.at[pl.ds(pl.multiple_of(g * cape, cape), cape), pl.ds(h * VH, VH)]

        @pl.loop(1, groups)
        def _(k):
            e = group_peer(groups - k, g, groups)
            pltpu.make_async_remote_copy(
                src_ref=disp.at[h, pl.ds(pl.multiple_of(e * cape, cape), cape)], dst_ref=spot,
                send_sem=disp_ssem.at[h], recv_sem=disp_rsem.at[h],
                device_id=(e, m), device_id_type=MESH,
            ).start()

        pltpu.make_async_copy(
            disp.at[h, pl.ds(pl.multiple_of(g * cape, cape), cape)], spot, own_sem.at[h]
        ).start()

    attend(0)
    send_latents(0)
    ring_pass(2, 0)
    attend(1)
    send_latents(1)
    ring_pass(2, 1)
    attend(2)
    send_latents(2)
    twin_wait(0)
    project(0)
    attend(3)
    send_latents(3)
    project(1)
    dispatch(0)
    twin_wait(1)
    project(2)
    dispatch(1)
    project(3)
    dispatch(2)
    dispatch(3)

    wait_for(fresh_out.at[pl.ds(0, groups - 1)], fresh_ssem.at[0])
    for step in range(1, REACH + 1):
        for way in range(2):
            for ab in range(2):
                wait_for(piece(0, ab, core), ring_ssem.at[step - 1, way, ab])
                wait_for(piece(0, ab, core), twin_ssem.at[step - 1, way, ab])

    @pl.loop(0, heads)
    def _(h):
        wait_for(lat_out.at[h, pl.ds(0, nx - 1), pl.ds(0, near_slots)], lat_ssem.at[h])
        wait_for(lat_out.at[h, pl.ds(0, nx), pl.ds(0, 3)], side_ssem.at[h])
        wait_for(val_out.at[h, pl.ds(0, nz - 1)], val_ssem.at[h])
        wait_for(disp.at[h, pl.ds(0, (groups - 1) * cape)], disp_ssem.at[h])
        wait_for(disp.at[h, pl.ds(0, (groups - 1) * cape)], disp_rsem.at[h])
        wait_for(disp.at[h, pl.ds(0, cape)], own_sem.at[h])


def local(cache, cache_len, query, fresh, fresh_dest, fresh_slot, token_group, w_uv):
    groups, members = lax.axis_size("group"), lax.axis_size("member")
    count, qtok, all_heads = query.shape[:3]
    rows = qtok * all_heads
    heads = w_uv.shape[0]
    n = fresh.shape[0]
    cap = 2 * n // groups
    tokens = token_group.shape[0]
    cape = 2 * tokens // groups
    mine = count * qtok
    block = rows * count // heads
    nx = 4
    nz = members // nx
    anywhere = pl.BlockSpec(memory_space=pl.ANY)
    dma = pltpu.SemaphoreType.DMA
    return pl.pallas_call(
        functools.partial(kernel, groups, members),
        out_shape=jax.ShapeDtypeStruct((groups * cape, heads * VH), BF16),
        in_specs=[anywhere] * 8,
        out_specs=anywhere,
        scratch_shapes=[
            pltpu.SMEM((count,), jnp.int32),
            pltpu.VMEM((1, n), jnp.int32),
            pltpu.VMEM((1, n), jnp.int32),
            pltpu.VMEM((1, tokens), jnp.int32),
            pltpu.VMEM((WIDTH, n), BF16),
            pltpu.VMEM((count, WIDTH, cache.shape[1]), BF16),
            pltpu.VMEM((count, qtok, WIDTH, all_heads), BF16),
            pltpu.VMEM((2 * REACH + 1,) + w_uv.shape, BF16),
            pltpu.VMEM((groups, cap, WIDE), BF16),
            pltpu.VMEM((groups, cap, WIDE), BF16),
            pltpu.VMEM((heads, block, WIDTH), BF16),
            pltpu.VMEM((heads, block, 1), F32),
            pltpu.VMEM((heads, block, 1), F32),
            pltpu.VMEM((heads, block, KVL), F32),
            pltpu.VMEM((block, groups * cap), F32),
            pltpu.VMEM((groups * cape, tokens), BF16),
            pltpu.VMEM((rows, rows), BF16),
            pltpu.VMEM((heads, nx, nz, 2 * mine, KVL // 2), BF16),
            pltpu.VMEM((heads, nx, nz, 2 * mine, KVL // 2), BF16),
            pltpu.VMEM((heads, nz, nx * mine, VH), BF16),
            pltpu.VMEM((heads, nz, nx * mine, VH), BF16),
            pltpu.VMEM((heads, groups * cape, VH), BF16),
            dma((6 + 2 * count,)),
            dma((1,)),
            dma((1,)),
            dma((REACH, 2, 2)),
            dma((REACH, 2, 2)),
            dma((REACH, 2, 2)),
            dma((REACH, 2, 2)),
            dma((heads,)),
            dma((heads,)),
            dma((heads,)),
            dma((heads,)),
            dma((heads,)),
            dma((heads,)),
            dma((heads,)),
            dma((heads,)),
            dma((heads,)),
        ],
        compiler_params=pltpu.CompilerParams(
            collective_id=0, has_side_effects=True, vmem_limit_bytes=60 * 1024 * 1024
        ),
        cost_estimate=pl.CostEstimate(flops=2_500_000_000, bytes_accessed=6_000_000, transcendentals=800_000),
    )(
        cache_len,
        fresh_dest.reshape(1, n),
        fresh_slot.reshape(1, n),
        token_group.reshape(1, tokens),
        fresh.T,
        cache.transpose(0, 2, 1),
        query.transpose(0, 1, 3, 2),
        w_uv,
    )


def solution(mesh):
    placed = (
        P(("group", "member"), None, None),
        P(("group", "member")),
        P(("group", "member"), None, None, None),
        P(("group", "member"), None),
        P(("group", "member"), None),
        P(("group", "member")),
        P("group", None),
        P("member", None, None),
    )
    return jax.shard_map(
        local, mesh=mesh, in_specs=placed, out_specs=P("group", "member"), check_vma=False
    )
```

```python
import functools

import jax
import jax.numpy as jnp
from jax import lax
from jax.experimental import pallas as pl
from jax.experimental.pallas import tpu as pltpu
from jax.sharding import PartitionSpec as P

KVL = 512
ROPE = 64
NOPE = 128
VH = 128
WIDTH = KVL + ROPE
WIDE = 640
SCALE = (NOPE + ROPE) ** (-0.5)
MESH = pl.DeviceIdType.MESH
F32 = jnp.float32
BF16 = jnp.bfloat16
REACH = 2
NT = (((1,), (1,)), ((), ()))


def iota(shape, axis):
    return lax.broadcasted_iota(jnp.int32, shape, axis)


def swing(j):
    return ((j + 1) >> 1) * (2 * (j & 1) - 1)


def group_peer(k, g, groups):
    return ((((g >> 1) + swing(k >> 1)) & (groups // 2 - 1)) << 1) | ((g ^ k) & 1)


def one_hot_places(targets, peers, cap):
    n = targets.shape[1]
    named = iota((peers, n), 0) == targets
    earlier = (iota((n, n), 0) < iota((n, n), 1)).astype(BF16)
    counts = jnp.dot(named.astype(BF16), earlier, preferred_element_type=F32)
    slot = jnp.sum(jnp.where(named, counts, 0.0), 0, keepdims=True)
    where_to = targets * cap + slot.astype(jnp.int32)
    return (iota((peers * cap, n), 0) == where_to).astype(BF16)


def kernel(
    groups, members, lens_hbm, dest_hbm, slot_hbm, tok_hbm, fresh_hbm, cache_hbm, query_hbm, w_hbm,
    out_ref,
    lens, dest, slot, tok, fresh, cache, query, weights, fresh_out, arrived, queries, top, total, near,
    bias, picks, back, lat_out, lat_in, val_out, val_in, disp,
    in_sem, fresh_ssem, fresh_rsem, ring_ssem, ring_rsem, twin_ssem, twin_rsem,
    lat_ssem, lat_rsem, side_ssem, side_rsem, val_ssem, val_rsem, disp_ssem, disp_rsem, own_sem,
):
    g, m = lax.axis_index("group"), lax.axis_index("member")
    count, keys = cache_hbm.shape[0], cache_hbm.shape[2]
    qtok = query_hbm.shape[1]
    rows = qtok * query_hbm.shape[3]
    heads = w_hbm.shape[0]
    part = rows // heads
    mine = count * qtok
    cap = fresh_out.shape[1]
    cape = disp.shape[1] // groups
    nx = 4
    nz = members // nx
    z, x, core = m >> 2, m & 3, g & 1
    half = KVL // 2
    pair = heads // 2

    def at_z(k):
        return (((z + k) & (nz - 1)) << 2) | x

    def at_x(k):
        return (z << 2) | ((x + k) & 3)

    def load(src, dst, i):
        return pltpu.make_async_copy(src, dst, in_sem.at[i])

    small = [
        load(fresh_hbm, fresh, 0), load(dest_hbm, dest, 1), load(slot_hbm, slot, 2),
        load(tok_hbm, tok, 3), load(lens_hbm, lens, 4),
    ]
    load_w = load(w_hbm, weights.at[REACH], 5)
    queries_in = [load(query_hbm.at[b], query.at[b], 6 + b) for b in range(count)]
    cache_in = [load(cache_hbm.at[b], cache.at[b], 6 + count + b) for b in range(count)]
    barrier = pltpu.get_barrier_semaphore()

    @pl.loop(1, groups)
    def _(k):
        pl.semaphore_signal(barrier, inc=1, device_id=(group_peer(groups - k, g, groups), m), device_id_type=MESH)

    @pl.loop(1, nz)
    def _(k):
        pl.semaphore_signal(barrier, inc=1, device_id=(g, at_z(k)), device_id_type=MESH)

    @pl.loop(1, nx)
    def _(k):
        pl.semaphore_signal(barrier, inc=1, device_id=(g, at_x(k)), device_id_type=MESH)
        for step in (-2, -1, 1, 2):
            aside = (at_z(step) & ~3) | ((x + k) & 3)
            pl.semaphore_signal(barrier, inc=1, device_id=(g, aside), device_id_type=MESH)

    for copy in small:
        copy.start()
    load_w.start()
    for b in range(count):
        queries_in[b].start()
        cache_in[b].start()
    for copy in small:
        copy.wait()

    places = one_hot_places(dest[...], groups, cap)
    fresh_out[:, :, :WIDTH] = (
        lax.dot_general(places, fresh[...], NT, preferred_element_type=F32)
        .astype(BF16)
        .reshape(groups, cap, WIDTH)
    )
    n = fresh.shape[1]
    marks = (iota((128, n), 0) - 64 == slot[...]).astype(BF16)
    marked = lax.dot_general(places, marks, NT, preferred_element_type=F32)
    fresh_out[:, :, WIDTH:] = marked[:, 64:].astype(BF16).reshape(groups, cap, WIDE - WIDTH)

    pl.semaphore_wait(barrier, groups - 1 + nz - 1 + 5 * (nx - 1))

    @pl.loop(1, groups)
    def _(k):
        e = group_peer(jnp.where(k <= groups // 2, groups + 1 - 2 * k, 2 * (groups - k)), g, groups)
        pltpu.make_async_remote_copy(
            src_ref=fresh_out.at[e], dst_ref=arrived.at[g],
            send_sem=fresh_ssem.at[0], recv_sem=fresh_rsem.at[0],
            device_id=(e, m), device_id_type=MESH,
        ).start()

    arrived[g] = fresh_out[g]

    def piece(k, ab, side):
        return weights.at[
            REACH + k, pl.ds(ab * pair, pair), pl.ds(pl.multiple_of(side * half, half), half)
        ]

    def ring_copy(step, way, ab):
        sign = 1 - 2 * way
        return pltpu.make_async_remote_copy(
            src_ref=piece(-sign * (step - 1), ab, core), dst_ref=piece(-sign * step, ab, core),
            send_sem=ring_ssem.at[step - 1, way, ab], recv_sem=ring_rsem.at[step - 1, way, ab],
            device_id=(g, at_z(sign)), device_id_type=MESH,
        )

    def twin_copy(step, way, ab):
        sign = 1 - 2 * way
        return pltpu.make_async_remote_copy(
            src_ref=piece(-sign * step, ab, core), dst_ref=piece(-sign * step, ab, core),
            send_sem=twin_ssem.at[step - 1, way, ab], recv_sem=twin_rsem.at[step - 1, way, ab],
            device_id=(g ^ 1, m), device_id_type=MESH,
        )

    def wait_for(ref, sem):
        pltpu.make_async_copy(ref, ref, sem).wait()

    def ring_pass(step, ab):
        for way in range(2):
            here = piece(-(1 - 2 * way) * step, ab, core)
            wait_for(here, ring_rsem.at[step - 1, way, ab])
            if step < REACH:
                ring_copy(step + 1, way, ab).start()
            twin_copy(step, way, ab).start()

    def twin_wait(ab):
        for step in range(1, REACH + 1):
            for way in range(2):
                there = piece(-(1 - 2 * way) * step, ab, 1 - core)
                wait_for(there, twin_rsem.at[step - 1, way, ab])

    load_w.wait()
    for ab in range(2):
        for way in range(2):
            ring_copy(1, way, ab).start()

    r, c = iota((rows, rows), 0), iota((rows, rows), 1)
    order = (lax.rem(r, qtok) * (rows // qtok) + lax.rem(r, part) // qtok * heads + r // part == c).astype(BF16)
    for b in range(count):
        queries_in[b].wait()
        cache_in[b].wait()
        columns = jnp.concatenate([query[b, i] for i in range(qtok)], 1)
        q = lax.dot_general(order, columns, NT, preferred_element_type=F32).astype(BF16)
        span = pl.ds(b * part, part)
        queries[:, span, :] = q.reshape(heads, part, WIDTH)
        score = jnp.dot(q, cache[b], preferred_element_type=F32) * SCALE
        score = jnp.where(iota((rows, keys), 1) < lens[b], score, -jnp.inf)
        high = jnp.max(score, -1, keepdims=True)
        p = jnp.exp(score - high)
        top[:, span, :] = high.reshape(heads, part, 1)
        total[:, span, :] = jnp.sum(p, -1, keepdims=True).reshape(heads, part, 1)
        near[:, span, :] = lax.dot_general(
            p.astype(BF16), cache[b, :KVL, :], NT, preferred_element_type=F32
        ).reshape(heads, part, KVL)

    picks[...] = one_hot_places(tok[...], groups, cape)
    r, c = iota((rows, rows), 0), iota((rows, rows), 1)
    whose = ((r // mine + z + nz // 2) & (nz - 1)) * nx + r // (mine * nz)
    back[...] = (lax.rem(r, mine) // qtok * part + whose * qtok + lax.rem(r, qtok) == c).astype(BF16)

    for ab in range(2):
        ring_pass(1, ab)

    wait_for(arrived.at[pl.ds(0, groups - 1)], fresh_rsem.at[0])
    pool = groups * cap
    chosen = (iota((8, 128), 1) - 64 == iota((8, 128), 0)).astype(BF16)
    labelled = lax.dot_general(
        chosen, arrived[:, :, KVL:].reshape(pool, WIDE - KVL), NT,
        preferred_element_type=F32,
    )
    for b in range(count):
        bias[b * part : (b + 1) * part, :] = jnp.broadcast_to(
            jnp.where(labelled[b : b + 1, :] > 0.5, 0.0, -jnp.inf), (part, pool)
        )

    def attend(h):
        keys_in = arrived[...].reshape(pool, WIDE)
        score = lax.dot_general(queries[h], keys_in[:, :WIDTH], NT, preferred_element_type=F32)
        score = score * SCALE + bias[...]
        high = jnp.maximum(top[h], jnp.max(score, -1, keepdims=True))
        p = jnp.exp(score - high)
        shrink = jnp.exp(top[h] - high)
        norm = 1.0 / (total[h] * shrink + jnp.sum(p, -1, keepdims=True))
        far = jnp.dot(p.astype(BF16), keys_in[:, :KVL], preferred_element_type=F32)
        latent = ((near[h] * shrink + far) * norm).astype(BF16)
        moved = jnp.dot(back[...], latent, preferred_element_type=F32).reshape(nx, nz, mine, KVL)
        lat_out[h] = jnp.concatenate([moved[..., :half], moved[..., half:]], 2).astype(BF16)

    near_slots = 2 * REACH + 1

    def far_way(h):
        return 1 - 2 * (h & 1)

    def send_latents(h):
        @pl.loop(0, nx)
        def _(k):
            to = (x + k) & 3
            for source, slot, step in ((0, 7, 2 * far_way(h)), (7, 5, 1), (1, 6, -1)):
                pltpu.make_async_remote_copy(
                    src_ref=lat_out.at[h, to, source], dst_ref=lat_in.at[h, x, slot],
                    send_sem=side_ssem.at[h], recv_sem=side_rsem.at[h],
                    device_id=(g, (((z + step) & (nz - 1)) << 2) | to), device_id_type=MESH,
                ).start()

        for k in (2, 1, 3):
            pltpu.make_async_remote_copy(
                src_ref=lat_out.at[h, (x + k) & 3, pl.ds(2, near_slots)],
                dst_ref=lat_in.at[h, x, pl.ds(0, near_slots)],
                send_sem=lat_ssem.at[h], recv_sem=lat_rsem.at[h],
                device_id=(g, at_x(k)), device_id_type=MESH,
            ).start()

        lat_in[h, x, :near_slots] = lat_out[h, x, 2 : 2 + near_slots]

    def project(h):
        wait_for(lat_in.at[h, pl.ds(0, nx - 1), pl.ds(0, near_slots)], lat_rsem.at[h])
        wait_for(lat_in.at[h, pl.ds(0, nx), pl.ds(0, 3)], side_rsem.at[h])
        way = far_way(h)
        plan = [(k, 0) for k in range(-REACH, REACH + 1)] + [(2, -1), (-2, 1), (2 * way, -2 * way)]
        for k in (REACH, -REACH, 1, -1, 0):
            slots = [i for i, (owner, _) in enumerate(plan) if owner == k]
            w = jnp.concatenate([weights[REACH + k, h, :half, :], weights[REACH + k, h, half:, :]], 1)
            taken = [lat_in[h, :, i].reshape(nx * 2 * mine, half) for i in slots]
            both = jnp.dot(
                jnp.concatenate(taken, 0), w, preferred_element_type=F32
            ).reshape(len(slots), nx, 2 * mine, 2 * VH)
            value = both[:, :, :mine, :VH] + both[:, :, mine:, VH:]
            for j, i in enumerate(slots):
                block = value[j].reshape(nx * mine, VH).astype(BF16)
                if k == 0:
                    val_in[h, z] = block
                    continue
                val_out[h, i] = block
                pltpu.make_async_remote_copy(
                    src_ref=val_out.at[h, i], dst_ref=val_in.at[h, (z + plan[i][1]) & (nz - 1)],
                    send_sem=val_ssem.at[h], recv_sem=val_rsem.at[h],
                    device_id=(g, at_z(k)), device_id_type=MESH,
                ).start()

    def dispatch(h):
        wait_for(val_in.at[h, pl.ds(0, nz - 1)], val_rsem.at[h])
        value = val_in[h].reshape(members * mine, VH)
        disp[h] = jnp.dot(picks[...], value, preferred_element_type=F32).astype(BF16)
        spot = out_ref.at[pl.ds(pl.multiple_of(g * cape, cape), cape), pl.ds(h * VH, VH)]

        @pl.loop(1, groups)
        def _(k):
            e = group_peer(jnp.where(k <= groups // 2, groups + 1 - 2 * k, 2 * (groups - k)), g, groups)
            pltpu.make_async_remote_copy(
                src_ref=disp.at[h, pl.ds(pl.multiple_of(e * cape, cape), cape)], dst_ref=spot,
                send_sem=disp_ssem.at[h], recv_sem=disp_rsem.at[h],
                device_id=(e, m), device_id_type=MESH,
            ).start()

        pltpu.make_async_copy(
            disp.at[h, pl.ds(pl.multiple_of(g * cape, cape), cape)], spot, own_sem.at[h]
        ).start()

    attend(0)
    send_latents(0)
    ring_pass(2, 0)
    attend(1)
    send_latents(1)
    ring_pass(2, 1)
    attend(2)
    send_latents(2)
    twin_wait(0)
    project(0)
    attend(3)
    send_latents(3)
    project(1)
    dispatch(0)
    twin_wait(1)
    project(2)
    dispatch(1)
    project(3)
    dispatch(2)
    dispatch(3)

    wait_for(fresh_out.at[pl.ds(0, groups - 1)], fresh_ssem.at[0])
    for step in range(1, REACH + 1):
        for way in range(2):
            for ab in range(2):
                wait_for(piece(0, ab, core), ring_ssem.at[step - 1, way, ab])
                wait_for(piece(0, ab, core), twin_ssem.at[step - 1, way, ab])

    @pl.loop(0, heads)
    def _(h):
        wait_for(lat_out.at[h, pl.ds(0, nx - 1), pl.ds(0, near_slots)], lat_ssem.at[h])
        wait_for(lat_out.at[h, pl.ds(0, nx), pl.ds(0, 3)], side_ssem.at[h])
        wait_for(val_out.at[h, pl.ds(0, nz - 1)], val_ssem.at[h])
        wait_for(disp.at[h, pl.ds(0, (groups - 1) * cape)], disp_ssem.at[h])
        wait_for(disp.at[h, pl.ds(0, (groups - 1) * cape)], disp_rsem.at[h])
        wait_for(disp.at[h, pl.ds(0, cape)], own_sem.at[h])


def local(cache, cache_len, query, fresh, fresh_dest, fresh_slot, token_group, w_uv):
    groups, members = lax.axis_size("group"), lax.axis_size("member")
    count, qtok, all_heads = query.shape[:3]
    rows = qtok * all_heads
    heads = w_uv.shape[0]
    n = fresh.shape[0]
    cap = 2 * n // groups
    tokens = token_group.shape[0]
    cape = 2 * tokens // groups
    mine = count * qtok
    block = rows * count // heads
    nx = 4
    nz = members // nx
    anywhere = pl.BlockSpec(memory_space=pl.ANY)
    dma = pltpu.SemaphoreType.DMA
    return pl.pallas_call(
        functools.partial(kernel, groups, members),
        out_shape=jax.ShapeDtypeStruct((groups * cape, heads * VH), BF16),
        in_specs=[anywhere] * 8,
        out_specs=anywhere,
        scratch_shapes=[
            pltpu.SMEM((count,), jnp.int32),
            pltpu.VMEM((1, n), jnp.int32),
            pltpu.VMEM((1, n), jnp.int32),
            pltpu.VMEM((1, tokens), jnp.int32),
            pltpu.VMEM((WIDTH, n), BF16),
            pltpu.VMEM((count, WIDTH, cache.shape[1]), BF16),
            pltpu.VMEM((count, qtok, WIDTH, all_heads), BF16),
            pltpu.VMEM((2 * REACH + 1,) + w_uv.shape, BF16),
            pltpu.VMEM((groups, cap, WIDE), BF16),
            pltpu.VMEM((groups, cap, WIDE), BF16),
            pltpu.VMEM((heads, block, WIDTH), BF16),
            pltpu.VMEM((heads, block, 1), F32),
            pltpu.VMEM((heads, block, 1), F32),
            pltpu.VMEM((heads, block, KVL), F32),
            pltpu.VMEM((block, groups * cap), F32),
            pltpu.VMEM((groups * cape, tokens), BF16),
            pltpu.VMEM((rows, rows), BF16),
            pltpu.VMEM((heads, nx, nz, 2 * mine, KVL // 2), BF16),
            pltpu.VMEM((heads, nx, nz, 2 * mine, KVL // 2), BF16),
            pltpu.VMEM((heads, nz, nx * mine, VH), BF16),
            pltpu.VMEM((heads, nz, nx * mine, VH), BF16),
            pltpu.VMEM((heads, groups * cape, VH), BF16),
            dma((6 + 2 * count,)),
            dma((1,)),
            dma((1,)),
            dma((REACH, 2, 2)),
            dma((REACH, 2, 2)),
            dma((REACH, 2, 2)),
            dma((REACH, 2, 2)),
            dma((heads,)),
            dma((heads,)),
            dma((heads,)),
            dma((heads,)),
            dma((heads,)),
            dma((heads,)),
            dma((heads,)),
            dma((heads,)),
            dma((heads,)),
        ],
        compiler_params=pltpu.CompilerParams(
            collective_id=0, has_side_effects=True, vmem_limit_bytes=60 * 1024 * 1024
        ),
        cost_estimate=pl.CostEstimate(flops=2_500_000_000, bytes_accessed=6_000_000, transcendentals=800_000),
    )(
        cache_len,
        fresh_dest.reshape(1, n),
        fresh_slot.reshape(1, n),
        token_group.reshape(1, tokens),
        fresh.T,
        cache.transpose(0, 2, 1),
        query.transpose(0, 1, 3, 2),
        w_uv,
    )


def solution(mesh):
    placed = (
        P(("group", "member"), None, None),
        P(("group", "member")),
        P(("group", "member"), None, None, None),
        P(("group", "member"), None),
        P(("group", "member"), None),
        P(("group", "member")),
        P("group", None),
        P("member", None, None),
    )
    return jax.shard_map(
        local, mesh=mesh, in_specs=placed, out_specs=P("group", "member"), check_vma=False
    )
```
